1024 devices in a mesh: dp: 16 (over x, y), group: 64 (over z, core).
Axes of the slice: x: 4, y: 4, z: 32, core: 2. Of those that a mesh axis runs over, the one named last changes fastest.
Arguments:
- grad_parts: bfloat16 [16, 64, 640, 640], P('dp', None, 'group'), may hold values from -0.29882812 to 0.29882812
- row_extent: int32 [64], replicated, may hold values from 384 to 640, as said below
- col_extent: int32 [64], replicated, may hold values from 384 to 640, as said below
- worker: int32 [64], replicated, may hold values from 0 to 63, as said below
- fact_left: float32 [128, 640, 640], P('group', 'dp'), as said below
- fact_right: float32 [128, 640, 640], P('group', 'dp'), as said below
- root_left: bfloat16 [128, 640, 640], P('group'), as said below
- root_right: bfloat16 [128, 640, 640], P('group'), as said below
Outputs:
- new_left: float32 [128, 640, 640], P('group', 'dp')
- new_right: float32 [128, 640, 640], P('group', 'dp')
- update: bfloat16 [128, 640, 640], P('group')
The draws below stay inside these ranges and needn't reach their ends.
Inputs may be any that keep to these rules, and one draw needn't show every extreme that they name: Each worker holds at most 2 blocks and some worker holds exactly 2; a worker that holds two blocks holds two blocks with a cut edge. `row_extent`: each entry is 384 or 640. `col_extent`: each entry is 384 or 640. `fact_left`: each slot is a symmetric matrix. `fact_right`: each slot is a symmetric matrix. `root_left`: each slot is a symmetric matrix. `root_right`: each slot is a symmetric matrix.
All inputs are finite; a program needn't handle non-finite values.
Results may differ from the reference program's by a relative error of at most 0.02.
Values may be sent and summed in bfloat16 or wider, within the bound.
A program may use at most 32 MiB of HBM per device.

```python
import math
import jax
import jax.numpy as jnp
from jax import lax

B = 640
EDGE = 384
CAP = 2
NBLK = 64
N_DP = 16
N_GROUP = 64


def block_layout(key):
    subkeys = jax.random.split(key, 3)
    sequence = jax.random.permutation(subkeys[0], NBLK)
    workers = jax.random.permutation(subkeys[1], N_GROUP)
    pair_count = NBLK // 4
    position = jnp.argsort(sequence).astype(jnp.int32)
    is_cut = position < 2 * pair_count
    worker_pos = jnp.where(is_cut, position // 2, position - pair_count)
    owners = workers[worker_pos].astype(jnp.int32)
    offset = jax.random.randint(subkeys[2], (), 0, 3)
    cut_side = (position + offset) % 3
    rows_kept = jnp.where(is_cut & (cut_side != 1), EDGE, B).astype(jnp.int32)
    cols_kept = jnp.where(is_cut & (cut_side != 0), EDGE, B).astype(jnp.int32)
    return (owners, rows_kept, cols_kept)


def draw_worker(key, part):
    owners, rows_kept, cols_kept = block_layout(key)
    return owners


def draw_row_extent(key, part):
    owners, rows_kept, cols_kept = block_layout(key)
    return rows_kept


def draw_col_extent(key, part):
    owners, rows_kept, cols_kept = block_layout(key)
    return cols_kept


def symmetric_from(noise, diag_key, spread, lowest, highest):
    sym_part = 0.5 * spread * (noise + jnp.swapaxes(noise, 1, 2))
    diagonal = jnp.exp(jax.random.uniform(diag_key, noise.shape[:2], jnp.float32, math.log(lowest), math.log(highest)))
    return sym_part + diagonal[:, :, None] * jnp.eye(noise.shape[1], dtype=jnp.float32)[None, :, :]


def draw_fact_left(key, part):
    key = jax.random.fold_in(key, 11)
    shape_all = (CAP * N_GROUP, B, B)
    noise = jax.random.normal(key, shape_all, jnp.float32)
    return symmetric_from(noise, jax.random.fold_in(key, 1), 1.0, 5.0, 50.0)


def draw_fact_right(key, part):
    key = jax.random.fold_in(key, 12)
    shape_all = (CAP * N_GROUP, B, B)
    noise = jax.random.normal(key, shape_all, jnp.float32)
    return symmetric_from(noise, jax.random.fold_in(key, 1), 1.0, 5.0, 50.0)


def draw_root_left(key, part):
    key = jax.random.fold_in(key, 13)
    shape_all = (CAP * N_GROUP, B, B)
    noise = jax.random.normal(key, shape_all, jnp.float32)
    return symmetric_from(noise, jax.random.fold_in(key, 1), 0.05, 1.0, 4.0).astype(jnp.bfloat16)


def draw_root_right(key, part):
    key = jax.random.fold_in(key, 14)
    shape_all = (CAP * N_GROUP, B, B)
    noise = jax.random.normal(key, shape_all, jnp.float32)
    return symmetric_from(noise, jax.random.fold_in(key, 1), 0.05, 1.0, 4.0).astype(jnp.bfloat16)


def levels(stream_key, shape, cuts, smallest, top_value):
    loudness, own = 1.0, jax.random.fold_in(stream_key, 6)
    for dim, shards_of in cuts:
        heights = jnp.exp(jax.random.uniform(jax.random.fold_in(own, dim), (shards_of,), jnp.float32, smallest / len(cuts), top_value / len(cuts)))
        loudness = loudness * jnp.repeat(heights, shape[dim] // shards_of).reshape([-1 if axis == dim else 1 for axis in range(len(shape))])
    return loudness


def normal_values(key, extent, width, limit, cuts=(), held_as=jnp.bfloat16):
    gain = levels(key, extent, cuts, -0.22, 0.18) if cuts else 1.0
    result = jax.random.normal(key, extent, jnp.float32) * width * gain
    return jnp.minimum(jnp.maximum(result, -limit), limit).astype(held_as)


def setup_inputs(seed: int = 0) -> dict:
    key_of = jax.random.split(jax.random.key(seed), 9)
    return {
        "grad_parts": normal_values(key_of[0], (N_DP, NBLK, B, B), 0.05, 0.29882812, ((0, 16), (2, 64))),
        "row_extent": draw_row_extent(jax.random.fold_in(key_of[8], 71), 0),
        "col_extent": draw_col_extent(jax.random.fold_in(key_of[8], 71), 0),
        "worker": draw_worker(jax.random.fold_in(key_of[8], 71), 0),
        "fact_left": draw_fact_left(jax.random.fold_in(key_of[8], 71), 0),
        "fact_right": draw_fact_right(jax.random.fold_in(key_of[8], 71), 0),
        "root_left": draw_root_left(jax.random.fold_in(key_of[8], 71), 0),
        "root_right": draw_root_right(jax.random.fold_in(key_of[8], 71), 0),
    }


def reference(grad_parts, row_extent, col_extent, worker, fact_left, fact_right, root_left, root_right):
    def add_replica(replica, running):
        return running + grad_parts[replica].astype(jnp.float32)

    grad_total = lax.fori_loop(0, N_DP, add_replica, jnp.zeros(grad_parts.shape[1:], jnp.float32))
    grad_sum = grad_total.astype(jnp.bfloat16)
    block_ids = jnp.arange(NBLK, dtype=jnp.int32)
    earlier = (worker[:, None] == worker[None, :]) & (block_ids[None, :] < block_ids[:, None])
    slot_index = (worker * CAP + jnp.sum(earlier.astype(jnp.int32), axis=1)).astype(jnp.int32)
    position = jnp.arange(B, dtype=jnp.int32)

    def block_step(block):
        inside = (position[:, None] < row_extent[block]) & (position[None, :] < col_extent[block])
        grad_block = jnp.where(inside, grad_sum[block], jnp.zeros((), jnp.bfloat16))
        left_term = jnp.dot(grad_block, grad_block.T, preferred_element_type=jnp.float32)
        right_term = jnp.dot(grad_block.T, grad_block, preferred_element_type=jnp.float32)
        mixed_grad = jnp.dot(grad_block, root_right[slot_index[block]], preferred_element_type=jnp.float32).astype(jnp.bfloat16)
        product = jnp.dot(root_left[slot_index[block]], mixed_grad, preferred_element_type=jnp.float32)
        product = jnp.where(inside, product, jnp.zeros((), jnp.float32)).astype(jnp.bfloat16)
        return left_term, right_term, product

    left_terms, right_terms, products = lax.map(block_step, block_ids)
    new_left = fact_left.at[slot_index].add(left_terms)
    new_right = fact_right.at[slot_index].add(right_terms)
    update = jnp.zeros(root_left.shape, jnp.bfloat16).at[slot_index].set(products)
    return new_left, new_right, update
```

```python
import functools

import jax
import jax.numpy as jnp
from jax import lax
from jax.experimental import pallas as pl
from jax.experimental.pallas import tpu as pltpu
from jax.sharding import PartitionSpec as P

MESH = pl.DeviceIdType.MESH
LANES = 128
PAIR = 2
ROW_GROUPS = 3
RING = 4
VMEM_BYTES = 60 * 1024 * 1024


def exchange_kernel(
    sizes,
    worker_hbm,
    grad_ref,
    full_ref,
    worker_ref,
    recv_ref,
    slot_ref,
    chosen_ref,
    worker_sem,
    rs_send,
    rs_recv,
    z_send,
    z_recv,
    ag_send,
    ag_recv,
):
    ranks, groups, blocks, pairs, tiles = sizes
    pieces = tiles * ROW_GROUPS
    slots = full_ref.shape[1]
    my_rank = lax.axis_index("dp")
    my_group = lax.axis_index("group")
    pltpu.make_async_copy(worker_hbm, worker_ref, worker_sem).start()
    barrier = pltpu.get_barrier_semaphore()

    def greet_rank(step, carry):
        pl.semaphore_signal(
            barrier,
            inc=1,
            device_id=(lax.rem(my_rank + step, ranks), my_group),
            device_id_type=MESH,
        )
        return carry

    def greet_group(step, carry):
        pl.semaphore_signal(
            barrier,
            inc=1,
            device_id=(my_rank, lax.rem(my_group + step, groups)),
            device_id_type=MESH,
        )
        return carry

    lax.fori_loop(1, ranks, greet_rank, 0)
    lax.fori_loop(1, groups, greet_group, 0)

    pl.semaphore_wait(barrier, ranks + groups - 2)

    def piece_rows(rank, half):
        first = PAIR * (2 * lax.rem(rank, ROW_GROUPS) + half)
        lanes = pl.multiple_of((rank // ROW_GROUPS) * LANES, LANES)
        return grad_ref.at[pl.ds(first, PAIR), :, pl.ds(lanes, LANES)]

    def when_held(rank, half, act):
        held = rank < pieces
        if half:
            held = held & (lax.rem(rank, ROW_GROUPS) < ROW_GROUPS - 1)

        @pl.when(held)
        def _():
            act()

    def scatter_each(half, act):
        def step_to(step, carry):
            target = lax.rem(my_rank + step, ranks)

            def go():
                act(
                    pltpu.make_async_remote_copy(
                        src_ref=piece_rows(target, half),
                        dst_ref=recv_ref.at[half, my_rank],
                        send_sem=rs_send.at[half, target],
                        recv_sem=rs_recv.at[half, my_rank],
                        device_id=(target, my_group),
                        device_id_type=MESH,
                    )
                )

            when_held(target, half, go)
            return carry

        lax.fori_loop(1, ranks, step_to, 0)

    halves = range(2)
    for half in halves:
        scatter_each(half, lambda copy: copy.start())
        own = pltpu.make_async_copy(
            piece_rows(my_rank, half), recv_ref.at[half, my_rank], rs_recv.at[half, my_rank]
        )
        when_held(my_rank, half, own.start)

    depth = PAIR * blocks
    place_rows = PAIR * slots * groups

    def lay_out_places():
        lane = lax.broadcasted_iota(jnp.int32, (8, depth), 1)
        block_of = lax.rem(lane, blocks)

        def lay_out(block, held_by):
            return jnp.where(block_of == block, worker_ref[block], held_by)

        held_by = lax.fori_loop(0, blocks, lay_out, jnp.zeros_like(lane), unroll=8)

        def count_earlier(block, order):
            same = (held_by == worker_ref[block]) & (block_of > block)
            return order + same.astype(jnp.int32)

        order = lax.fori_loop(0, blocks, count_earlier, jnp.zeros_like(lane), unroll=8)
        place = PAIR * (slots * held_by + order) + lane // blocks
        row = lax.broadcasted_iota(jnp.int32, (place_rows, depth), 0)
        chosen_ref[...] = jnp.where(row == place[0:1], 1.0, 0.0).astype(jnp.bfloat16)

    pltpu.make_async_copy(worker_hbm, worker_ref, worker_sem).wait()
    when_held(my_rank, 0, lay_out_places)

    def spread_copy(half, target):
        return pltpu.make_async_remote_copy(
            src_ref=slot_ref.at[half, target],
            dst_ref=landing(half),
            send_sem=z_send.at[half],
            recv_sem=z_recv.at[half],
            device_id=(my_rank, target),
            device_id_type=MESH,
        )

    def pair_of(rank, half):
        return 2 * lax.rem(rank, ROW_GROUPS) + half

    def landing(half):
        return full_ref.at[
            my_rank // ROW_GROUPS, :, my_group, pair_of(my_rank, half)
        ]

    def spread(half):
        total = jnp.zeros((PAIR, blocks, LANES), jnp.float32)
        for step in range(ranks):
            source = lax.rem(my_rank + (ranks - step), ranks)
            arrived = recv_ref.at[half, source]
            pltpu.make_async_copy(arrived, arrived, rs_recv.at[half, source]).wait()
            total = total + recv_ref[half, source].astype(jnp.float32)
        total = total.reshape(depth, LANES).astype(jnp.bfloat16)
        placed = jnp.dot(chosen_ref[...], total, preferred_element_type=jnp.float32)
        slot_ref.at[half].reshape(place_rows, LANES)[...] = placed.astype(jnp.bfloat16)

        def spread_start(hop, carry):
            reach = groups // 2 - (hop + 1) // 2
            target = lax.rem(
                my_group + jnp.where(lax.rem(hop, 2) == 0, reach, groups - reach), groups
            )
            spread_copy(half, target).start()
            return carry

        lax.fori_loop(0, groups - 1, spread_start, 0)
        pltpu.make_async_copy(
            slot_ref.at[half, my_group], landing(half), z_recv.at[half]
        ).start()

    def spread_wait(half):
        mine = full_ref.at[my_rank // ROW_GROUPS, :, :, pair_of(my_rank, half)]
        pltpu.make_async_copy(mine, mine, z_recv.at[half]).wait()

    def spread_finish(half):
        sent = slot_ref.at[half, pl.ds(0, groups - 1)]
        pltpu.make_async_copy(sent, sent, z_send.at[half]).wait()

    for half in halves:
        when_held(my_rank, half, functools.partial(spread, half))

    side = RING
    my_x, my_y = my_rank // side, lax.rem(my_rank, side)
    chunks = [(slot, half) for half in halves for slot in range(slots)]

    def rank_at(slot, first, second):
        first, second = lax.rem(first, side), lax.rem(second, side)
        return side * first + second if slot == 0 else side * second + first

    def relay_copy(slot, half, source, target, index):
        piece = full_ref.at[
            source // ROW_GROUPS, slot, :, pair_of(source, half)
        ]
        return pltpu.make_async_remote_copy(
            src_ref=piece,
            dst_ref=piece,
            send_sem=ag_send.at[slot, half, index],
            recv_sem=ag_recv.at[slot, half, source],
            device_id=(target, my_group),
            device_id_type=MESH,
        )

    def relays(slot, half):
        first, second = (my_x, my_y) if slot == 0 else (my_y, my_x)
        at = functools.partial(rank_at, slot)
        ahead = (slot + half) % 2 == 0
        onward = (side - 1, 1) if ahead else (1, side - 1)
        lines = (0, 1, side - 1, side // 2)
        moves = {"own": [], "near": [], "far": [], "cross": [], "last": []}
        me = at(first, second)
        moves["own"] = [
            (me, at(first + 1, second)),
            (me, at(first + side - 1, second)),
            (me, at(first, second + 1)),
            (me, at(first, second + side - 1)),
        ]
        for line in (1, side - 1):
            source = at(first + line, second)
            targets = [at(first, second + 1), at(first, second + side - 1)]
            if line == onward[0]:
                targets = [at(first + onward[1], second)] + targets
            moves["near"].append((source, targets))
        source = at(first + side // 2, second)
        moves["far"].append((source, [at(first, second + 1), at(first, second + side - 1)]))
        for line in lines:
            for turn in (1, side - 1):
                source = at(first + line, second + turn)
                targets = [at(first, second + onward[1])] if turn == onward[0] else []
                moves["cross"].append((source, targets))
            moves["last"].append((at(first + line, second + side // 2), []))
        return moves

    plans = {chunk: relays(*chunk) for chunk in chunks}
    started = {chunk: [] for chunk in chunks}

    def relay_start(slot, half, source, targets):
        sends = []
        for target in targets:
            index = len(started[slot, half])
            started[slot, half].append((source, target))
            sends.append(relay_copy(slot, half, source, target, index))
        when_held(source, half, lambda: [copy.start() for copy in sends])

    def relay_own(half):
        for slot in range(slots):
            moves = plans[slot, half]["own"]
            relay_start(slot, half, moves[0][0], [target for _, target in moves])

    def relay_on(stage, half):
        for slot in range(slots):
            for source, targets in plans[slot, half][stage]:
                arrival = relay_copy(slot, half, source, my_rank, 0)
                when_held(source, half, arrival.wait_recv)
                if targets:
                    relay_start(slot, half, source, targets)

    when_held(my_rank, 0, lambda: spread_wait(0))
    relay_own(0)
    relay_on("near", 0)
    when_held(my_rank, 1, lambda: spread_wait(1))
    relay_own(1)
    for stage, half in (
        ("far", 0),
        ("near", 1),
        ("cross", 0),
        ("far", 1),
        ("cross", 1),
        ("last", 0),
        ("last", 1),
    ):
        relay_on(stage, half)

    for half in halves:
        scatter_each(half, lambda copy: copy.wait_send())
        when_held(my_rank, half, functools.partial(spread_finish, half))
    for slot, half in chunks:
        for index, (source, target) in enumerate(started[slot, half]):
            sent = relay_copy(slot, half, source, target, index)
            when_held(source, half, sent.wait_send)


def exchange(grad, worker, sizes):
    ranks, groups, blocks, pairs, tiles = sizes
    slots = 2
    return pl.pallas_call(
        functools.partial(exchange_kernel, sizes),
        out_shape=jax.ShapeDtypeStruct(
            (tiles, slots, groups, pairs, PAIR, LANES), jnp.bfloat16
        ),
        in_specs=[
            pl.BlockSpec(memory_space=pl.ANY),
            pl.BlockSpec(memory_space=pl.ANY),
        ],
        out_specs=pl.BlockSpec(memory_space=pltpu.VMEM),
        scratch_shapes=[
            pltpu.SMEM((blocks,), jnp.int32),
            pltpu.VMEM((2, ranks, PAIR, blocks, LANES), jnp.bfloat16),
            pltpu.VMEM((2, groups, slots, PAIR, LANES), jnp.bfloat16),
            pltpu.VMEM((PAIR * slots * groups, PAIR * blocks), jnp.bfloat16),
            pltpu.SemaphoreType.DMA,
            pltpu.SemaphoreType.DMA((2, ranks)),
            pltpu.SemaphoreType.DMA((2, ranks)),
            pltpu.SemaphoreType.DMA((2,)),
            pltpu.SemaphoreType.DMA((2,)),
            pltpu.SemaphoreType.DMA((slots, 2, ranks)),
            pltpu.SemaphoreType.DMA((slots, 2, ranks)),
        ],
        compiler_params=pltpu.CompilerParams(
            collective_id=0, has_side_effects=True, vmem_limit_bytes=VMEM_BYTES
        ),
    )(worker, grad)


def update_kernel(
    worker_ref,
    row_extent_ref,
    col_extent_ref,
    full_ref,
    fact_left_ref,
    fact_right_ref,
    root_left_ref,
    root_right_ref,
    new_left_ref,
    new_right_ref,
    update_ref,
    grad_ref,
):
    slot = pl.program_id(0)
    my_rank = lax.axis_index("dp")
    my_group = lax.axis_index("group")
    blocks = worker_ref.shape[0]
    tiles, _, groups, pairs, _, _ = full_ref.shape
    size = root_left_ref.shape[1]
    own = fact_left_ref.shape[1]

    def find(block, carry):
        seen, rows, cols = carry
        mine = worker_ref[block] == my_group
        hit = mine & (seen == slot)
        rows = jnp.where(hit, row_extent_ref[block], rows)
        cols = jnp.where(hit, col_extent_ref[block], cols)
        return seen + mine.astype(jnp.int32), rows, cols

    zero = jnp.int32(0)
    _, row_limit, col_limit = lax.fori_loop(0, blocks, find, (zero, zero, zero), unroll=True)

    row = lax.broadcasted_iota(jnp.int32, (size, LANES), 0)
    lane = lax.broadcasted_iota(jnp.int32, (size, LANES), 1)
    for tile in range(tiles):
        part = full_ref.at[tile, 0].reshape(size, LANES)[...]
        inside = (row < row_limit) & (tile * LANES + lane < col_limit)
        grad_ref[:, tile * LANES : (tile + 1) * LANES] = jnp.where(
            inside, part.astype(jnp.float32), 0.0
        ).astype(jnp.bfloat16)
    grad = grad_ref[...]

    mixed = jnp.dot(grad, root_right_ref[0], preferred_element_type=jnp.float32)
    product = jnp.dot(
        root_left_ref[0], mixed.astype(jnp.bfloat16), preferred_element_type=jnp.float32
    )
    out_row = lax.broadcasted_iota(jnp.int32, (size, size), 0)
    out_col = lax.broadcasted_iota(jnp.int32, (size, size), 1)
    inside = (out_row < row_limit) & (out_col < col_limit)
    update_ref[0] = jnp.where(inside, product, 0.0).astype(jnp.bfloat16)

    start = my_rank * own
    pick = lax.broadcasted_iota(jnp.int32, (size, LANES), 0) == start + lane
    pick = jnp.where(pick & (lane < own), 1.0, 0.0).astype(jnp.bfloat16)
    own_cols = jnp.dot(grad, pick, preferred_element_type=jnp.float32).astype(jnp.bfloat16)
    own_rows = lax.dot_general(
        pick, grad, (((0,), (0,)), ((), ())), preferred_element_type=jnp.float32
    ).astype(jnp.bfloat16)
    left = lax.dot_general(
        own_rows, grad, (((1,), (1,)), ((), ())), preferred_element_type=jnp.float32
    )
    right = lax.dot_general(
        own_cols, grad, (((0,), (0,)), ((), ())), preferred_element_type=jnp.float32
    )
    new_left_ref[0] = fact_left_ref[0] + left[:own]
    new_right_ref[0] = fact_right_ref[0] + right[:own]


def precondition(full, worker, row_extent, col_extent, fact_left, fact_right, root_left, root_right):
    slots, own, size = fact_left.shape
    tiles, _, groups, pairs, _, _ = full.shape
    smem = pl.BlockSpec(memory_space=pltpu.SMEM)
    fact = pl.BlockSpec((1, own, size), lambda slot: (slot, 0, 0))
    root = pl.BlockSpec((1, size, size), lambda slot: (slot, 0, 0))
    return pl.pallas_call(
        update_kernel,
        grid=(slots,),
        out_shape=(
            jax.ShapeDtypeStruct(fact_left.shape, jnp.float32),
            jax.ShapeDtypeStruct(fact_right.shape, jnp.float32),
            jax.ShapeDtypeStruct(root_left.shape, jnp.bfloat16),
        ),
        in_specs=[
            smem,
            smem,
            smem,
            pl.BlockSpec(
                (tiles, 1, groups, pairs, PAIR, LANES), lambda slot: (0, slot, 0, 0, 0, 0)
            ),
            fact,
            fact,
            root,
            root,
        ],
        out_specs=(fact, fact, root),
        scratch_shapes=[pltpu.VMEM((size, size), jnp.bfloat16)],
        compiler_params=pltpu.CompilerParams(vmem_limit_bytes=VMEM_BYTES),
    )(worker, row_extent, col_extent, full, fact_left, fact_right, root_left, root_right)


def solution(mesh):
    placed = (
        P("dp", None, "group", None),
        P(),
        P(),
        P(),
        P("group", "dp", None),
        P("group", "dp", None),
        P("group", None, None),
        P("group", None, None),
    )

    def local(grad_parts, row_extent, col_extent, worker, fact_left, fact_right, root_left, root_right):
        grad = jnp.transpose(grad_parts[0], (1, 0, 2))
        rows, blocks, size = grad.shape
        sizes = (
            mesh.shape["dp"],
            mesh.shape["group"],
            blocks,
            rows // PAIR,
            size // LANES,
        )
        full = exchange(grad, worker, sizes)
        return precondition(
            full, worker, row_extent, col_extent, fact_left, fact_right, root_left, root_right
        )

    return jax.shard_map(
        local,
        mesh=mesh,
        in_specs=placed,
        out_specs=(P("group", "dp", None), P("group", "dp", None), P("group", None, None)),
        check_vma=False,
    )
```

```python
import functools

import jax
import jax.numpy as jnp
from jax import lax
from jax.experimental import pallas as pl
from jax.experimental.pallas import tpu as pltpu
from jax.sharding import PartitionSpec as P

MESH = pl.DeviceIdType.MESH
LANES = 128
PAIR = 2
ROW_GROUPS = 3
RING = 4
SQUARE = 8
VMEM_BYTES = 60 * 1024 * 1024


def split_rank(rank):
    tile = lax.div(rank * 11, 32)
    return tile, rank - ROW_GROUPS * tile


def exchange_kernel(
    sizes,
    worker_hbm,
    grad_ref,
    full_ref,
    worker_ref,
    recv_ref,
    slot_ref,
    chosen_ref,
    worker_sem,
    ready_sem,
    rs_send,
    rs_recv,
    z_send,
    z_recv,
    ag_send,
    ag_recv,
):
    ranks, groups, blocks, pairs, tiles = sizes
    pieces = tiles * ROW_GROUPS
    slots = full_ref.shape[1]
    my_rank = lax.axis_index("dp")
    my_group = lax.axis_index("group")
    pltpu.make_async_copy(worker_hbm, worker_ref, worker_sem).start()
    barrier = pltpu.get_barrier_semaphore()

    def greet_rank(step, carry):
        pl.semaphore_signal(
            barrier,
            inc=1,
            device_id=(lax.rem(my_rank + step, ranks), my_group),
            device_id_type=MESH,
        )
        return carry

    row_first = SQUARE * lax.div(my_group, SQUARE)
    place = lax.rem(my_group, SQUARE)

    def in_row(step):
        return row_first + lax.rem(place + step, SQUARE)

    def in_column(step):
        return lax.rem(my_group + SQUARE * step, groups)

    def signal(semaphore, member):
        pl.semaphore_signal(
            semaphore, inc=1, device_id=(my_rank, member), device_id_type=MESH
        )

    def greet_row(step, carry):
        signal(barrier, in_row(step))
        return carry

    rows = groups // SQUARE
    lax.fori_loop(1, ranks, greet_rank, 0)
    lax.fori_loop(1, SQUARE, greet_row, 0)
    signal(barrier, in_column(1))
    signal(barrier, in_column(rows - 1))
    pl.semaphore_wait(barrier, ranks + SQUARE)

    def piece_rows(rank, half):
        tile, row_group = split_rank(rank)
        first = PAIR * (2 * row_group + half)
        lanes = pl.multiple_of(tile * LANES, LANES)
        return grad_ref.at[pl.ds(first, PAIR), :, pl.ds(lanes, LANES)]

    def when_held(rank, half, act):
        held = rank < pieces
        if half:
            held = held & (split_rank(rank)[1] < ROW_GROUPS - 1)

        @pl.when(held)
        def _():
            act()

    def scatter_each(half, act):
        def step_to(step, carry):
            target = lax.rem(my_rank + step, ranks)

            def go():
                act(
                    pltpu.make_async_remote_copy(
                        src_ref=piece_rows(target, half),
                        dst_ref=recv_ref.at[half, my_rank],
                        send_sem=rs_send.at[half, target],
                        recv_sem=rs_recv.at[half, my_rank],
                        device_id=(target, my_group),
                        device_id_type=MESH,
                    )
                )

            when_held(target, half, go)
            return carry

        lax.fori_loop(1, ranks, step_to, 0)

    halves = range(2)
    def scatter_start(half):
        scatter_each(half, lambda copy: copy.start())
        own = pltpu.make_async_copy(
            piece_rows(my_rank, half), recv_ref.at[half, my_rank], rs_recv.at[half, my_rank]
        )
        when_held(my_rank, half, own.start)

    scatter_start(0)

    depth = PAIR * blocks
    place_rows = PAIR * slots * groups

    def lay_out_places():
        lane = lax.broadcasted_iota(jnp.int32, (8, depth), 1)
        block_of = lax.rem(lane, blocks)

        def lay_out(block, held_by):
            return jnp.where(block_of == block, worker_ref[block], held_by)

        held_by = lax.fori_loop(0, blocks, lay_out, jnp.zeros_like(lane), unroll=8)

        def count_earlier(block, order):
            same = (held_by == worker_ref[block]) & (block_of > block)
            return order + same.astype(jnp.int32)

        order = lax.fori_loop(0, blocks, count_earlier, jnp.zeros_like(lane), unroll=8)
        place = PAIR * (slots * held_by + order) + lane // blocks
        row = lax.broadcasted_iota(jnp.int32, (place_rows, depth), 0)
        chosen_ref[...] = jnp.where(row == place[0:1], 1.0, 0.0).astype(jnp.bfloat16)

    rounds = rows // 2

    def tell(index):
        signal(ready_sem.at[index], in_column(1))
        signal(ready_sem.at[index], in_column(rows - 1))

    def hear(index):
        pl.semaphore_wait(ready_sem.at[index], 2)

    tell(0)
    pltpu.make_async_copy(worker_hbm, worker_ref, worker_sem).wait()
    when_held(my_rank, 0, lay_out_places)
    for index in range(1, rounds):
        hear(index - 1)
        tell(index)
    scatter_each(0, lambda copy: copy.wait_send())
    scatter_start(1)

    def spread_copy(half, target):
        return pltpu.make_async_remote_copy(
            src_ref=slot_ref.at[half, target],
            dst_ref=landing(half),
            send_sem=z_send.at[half],
            recv_sem=z_recv.at[half],
            device_id=(my_rank, target),
            device_id_type=MESH,
        )

    def landing(half):
        tile, row_group = split_rank(my_rank)
        return full_ref.at[tile, :, my_group, 2 * row_group + half]

    def spread(half):
        total = jnp.zeros((PAIR, blocks, LANES), jnp.float32)
        for step in range(ranks):
            source = lax.rem(my_rank + (ranks - step), ranks)
            arrived = recv_ref.at[half, source]
            pltpu.make_async_copy(arrived, arrived, rs_recv.at[half, source]).wait()
            total = total + recv_ref[half, source].astype(jnp.float32)
        total = total.reshape(depth, LANES).astype(jnp.bfloat16)
        placed = jnp.dot(chosen_ref[...], total, preferred_element_type=jnp.float32)
        slot_ref.at[half].reshape(place_rows, LANES)[...] = placed.astype(jnp.bfloat16)

        def spread_start(hop, carry):
            reach = groups // 2 - (hop + 1) // 2
            target = lax.rem(
                my_group + jnp.where(lax.rem(hop, 2) == 0, reach, groups - reach), groups
            )
            spread_copy(half, target).start()
            return carry

        lax.fori_loop(0, groups - 1, spread_start, 0)
        pltpu.make_async_copy(
            slot_ref.at[half, my_group], landing(half), z_recv.at[half]
        ).start()

    def spread_wait(half):
        tile, row_group = split_rank(my_rank)
        mine = full_ref.at[tile, :, :, 2 * row_group + half]
        pltpu.make_async_copy(mine, mine, z_recv.at[half]).wait()

    def spread_finish(half):
        sent = slot_ref.at[half, pl.ds(0, groups - 1)]
        pltpu.make_async_copy(sent, sent, z_send.at[half]).wait()

    hear(rounds - 1)
    for half in halves:
        when_held(my_rank, half, functools.partial(spread, half))

    side = RING
    my_x, my_y = my_rank // side, lax.rem(my_rank, side)
    chunks = [(slot, half) for half in halves for slot in range(slots)]

    def rank_at(slot, first, second):
        first, second = lax.rem(first, side), lax.rem(second, side)
        return side * first + second if slot == 0 else side * second + first

    def relay_copy(slot, half, source, target, index):
        tile, row_group = split_rank(source)
        piece = full_ref.at[tile, slot, :, 2 * row_group + half]
        return pltpu.make_async_remote_copy(
            src_ref=piece,
            dst_ref=piece,
            send_sem=ag_send.at[slot, half, index],
            recv_sem=ag_recv.at[slot, half, source],
            device_id=(target, my_group),
            device_id_type=MESH,
        )

    def relays(slot, half):
        first, second = (my_x, my_y) if slot == 0 else (my_y, my_x)
        at = functools.partial(rank_at, slot)
        ahead = (slot + half) % 2 == 0
        onward = (side - 1, 1) if ahead else (1, side - 1)
        lines = (0, 1, side - 1, side // 2)
        moves = {"own": [], "near": [], "far": [], "cross": [], "last": []}
        me = at(first, second)
        moves["own"] = [
            (me, at(first + 1, second)),
            (me, at(first + side - 1, second)),
            (me, at(first, second + 1)),
            (me, at(first, second + side - 1)),
        ]
        for line in (1, side - 1):
            source = at(first + line, second)
            targets = [at(first, second + 1), at(first, second + side - 1)]
            if line == onward[0]:
                targets = [at(first + onward[1], second)] + targets
            moves["near"].append((source, targets))
        source = at(first + side // 2, second)
        moves["far"].append((source, [at(first, second + 1), at(first, second + side - 1)]))
        for line in lines:
            for turn in (1, side - 1):
                source = at(first + line, second + turn)
                targets = [at(first, second + onward[1])] if turn == onward[0] else []
                moves["cross"].append((source, targets))
            moves["last"].append((at(first + line, second + side // 2), []))
        return moves

    plans = {chunk: relays(*chunk) for chunk in chunks}
    started = {chunk: [] for chunk in chunks}

    def relay_start(slot, half, source, targets):
        sends = []
        for target in targets:
            index = len(started[slot, half])
            started[slot, half].append((source, target))
            sends.append(relay_copy(slot, half, source, target, index))
        when_held(source, half, lambda: [copy.start() for copy in sends])

    def relay_own(half):
        for slot in range(slots):
            moves = plans[slot, half]["own"]
            relay_start(slot, half, moves[0][0], [target for _, target in moves])

    def relay_on(stage, half):
        for slot in range(slots):
            for source, targets in plans[slot, half][stage]:
                arrival = relay_copy(slot, half, source, my_rank, 0)
                when_held(source, half, arrival.wait_recv)
                if targets:
                    relay_start(slot, half, source, targets)

    when_held(my_rank, 0, functools.partial(spread_wait, 0))
    relay_own(0)
    relay_on("near", 0)
    when_held(my_rank, 1, functools.partial(spread_wait, 1))
    relay_own(1)
    for stage, half in (
        ("far", 0),
        ("near", 1),
        ("cross", 0),
        ("far", 1),
        ("cross", 1),
        ("last", 0),
        ("last", 1),
    ):
        relay_on(stage, half)

    scatter_each(1, lambda copy: copy.wait_send())
    for half in halves:
        when_held(my_rank, half, functools.partial(spread_finish, half))
    for slot, half in chunks:
        for index, (source, target) in enumerate(started[slot, half]):
            sent = relay_copy(slot, half, source, target, index)
            when_held(source, half, sent.wait_send)


def exchange(grad, worker, sizes):
    ranks, groups, blocks, pairs, tiles = sizes
    slots = 2
    return pl.pallas_call(
        functools.partial(exchange_kernel, sizes),
        out_shape=jax.ShapeDtypeStruct(
            (tiles, slots, groups, pairs, PAIR, LANES), jnp.bfloat16
        ),
        in_specs=[
            pl.BlockSpec(memory_space=pl.ANY),
            pl.BlockSpec(memory_space=pl.ANY),
        ],
        out_specs=pl.BlockSpec(memory_space=pltpu.VMEM),
        scratch_shapes=[
            pltpu.SMEM((blocks,), jnp.int32),
            pltpu.VMEM((2, ranks, PAIR, blocks, LANES), jnp.bfloat16),
            pltpu.VMEM((2, groups, slots, PAIR, LANES), jnp.bfloat16),
            pltpu.VMEM((PAIR * slots * groups, PAIR * blocks), jnp.bfloat16),
            pltpu.SemaphoreType.DMA,
            pltpu.SemaphoreType.REGULAR((groups // SQUARE // 2,)),
            pltpu.SemaphoreType.DMA((2, ranks)),
            pltpu.SemaphoreType.DMA((2, ranks)),
            pltpu.SemaphoreType.DMA((2,)),
            pltpu.SemaphoreType.DMA((2,)),
            pltpu.SemaphoreType.DMA((slots, 2, ranks)),
            pltpu.SemaphoreType.DMA((slots, 2, ranks)),
        ],
        compiler_params=pltpu.CompilerParams(
            collective_id=0, has_side_effects=True, vmem_limit_bytes=VMEM_BYTES
        ),
    )(worker, grad)


def update_kernel(
    worker_ref,
    row_extent_ref,
    col_extent_ref,
    full_ref,
    fact_left_ref,
    fact_right_ref,
    root_left_ref,
    root_right_ref,
    new_left_ref,
    new_right_ref,
    update_ref,
    grad_ref,
):
    slot = pl.program_id(0)
    my_rank = lax.axis_index("dp")
    my_group = lax.axis_index("group")
    blocks = worker_ref.shape[0]
    tiles, _, groups, pairs, _, _ = full_ref.shape
    size = root_left_ref.shape[1]
    own = fact_left_ref.shape[1]

    def find(block, carry):
        seen, rows, cols = carry
        mine = worker_ref[block] == my_group
        hit = mine & (seen == slot)
        rows = jnp.where(hit, row_extent_ref[block], rows)
        cols = jnp.where(hit, col_extent_ref[block], cols)
        return seen + mine.astype(jnp.int32), rows, cols

    zero = jnp.int32(0)
    _, row_limit, col_limit = lax.fori_loop(0, blocks, find, (zero, zero, zero), unroll=True)

    row = lax.broadcasted_iota(jnp.int32, (size, LANES), 0)
    lane = lax.broadcasted_iota(jnp.int32, (size, LANES), 1)
    for tile in range(tiles):
        part = full_ref.at[tile, 0].reshape(size, LANES)[...]
        inside = (row < row_limit) & (tile * LANES + lane < col_limit)
        grad_ref[:, tile * LANES : (tile + 1) * LANES] = jnp.where(
            inside, part.astype(jnp.float32), 0.0
        ).astype(jnp.bfloat16)
    grad = grad_ref[...]

    mixed = jnp.dot(grad, root_right_ref[0], preferred_element_type=jnp.float32)
    product = jnp.dot(
        root_left_ref[0], mixed.astype(jnp.bfloat16), preferred_element_type=jnp.float32
    )
    out_row = lax.broadcasted_iota(jnp.int32, (size, size), 0)
    out_col = lax.broadcasted_iota(jnp.int32, (size, size), 1)
    inside = (out_row < row_limit) & (out_col < col_limit)
    update_ref[0] = jnp.where(inside, product, 0.0).astype(jnp.bfloat16)

    start = my_rank * own
    pick = lax.broadcasted_iota(jnp.int32, (size, LANES), 0) == start + lane
    pick = jnp.where(pick & (lane < own), 1.0, 0.0).astype(jnp.bfloat16)
    own_cols = jnp.dot(grad, pick, preferred_element_type=jnp.float32).astype(jnp.bfloat16)
    own_rows = lax.dot_general(
        pick, grad, (((0,), (0,)), ((), ())), preferred_element_type=jnp.float32
    ).astype(jnp.bfloat16)
    left = lax.dot_general(
        own_rows, grad, (((1,), (1,)), ((), ())), preferred_element_type=jnp.float32
    )
    right = lax.dot_general(
        own_cols, grad, (((0,), (0,)), ((), ())), preferred_element_type=jnp.float32
    )
    new_left_ref[0] = fact_left_ref[0] + left[:own]
    new_right_ref[0] = fact_right_ref[0] + right[:own]


def precondition(full, worker, row_extent, col_extent, fact_left, fact_right, root_left, root_right):
    slots, own, size = fact_left.shape
    tiles, _, groups, pairs, _, _ = full.shape
    smem = pl.BlockSpec(memory_space=pltpu.SMEM)
    fact = pl.BlockSpec((1, own, size), lambda slot: (slot, 0, 0))
    root = pl.BlockSpec((1, size, size), lambda slot: (slot, 0, 0))
    return pl.pallas_call(
        update_kernel,
        grid=(slots,),
        out_shape=(
            jax.ShapeDtypeStruct(fact_left.shape, jnp.float32),
            jax.ShapeDtypeStruct(fact_right.shape, jnp.float32),
            jax.ShapeDtypeStruct(root_left.shape, jnp.bfloat16),
        ),
        in_specs=[
            smem,
            smem,
            smem,
            pl.BlockSpec(
                (tiles, 1, groups, pairs, PAIR, LANES), lambda slot: (0, slot, 0, 0, 0, 0)
            ),
            fact,
            fact,
            root,
            root,
        ],
        out_specs=(fact, fact, root),
        scratch_shapes=[pltpu.VMEM((size, size), jnp.bfloat16)],
        compiler_params=pltpu.CompilerParams(vmem_limit_bytes=VMEM_BYTES),
    )(worker, row_extent, col_extent, full, fact_left, fact_right, root_left, root_right)


def solution(mesh):
    placed = (
        P("dp", None, "group", None),
        P(),
        P(),
        P(),
        P("group", "dp", None),
        P("group", "dp", None),
        P("group", None, None),
        P("group", None, None),
    )

    def local(grad_parts, row_extent, col_extent, worker, fact_left, fact_right, root_left, root_right):
        grad = jnp.transpose(grad_parts[0], (1, 0, 2))
        rows, blocks, size = grad.shape
        sizes = (
            mesh.shape["dp"],
            mesh.shape["group"],
            blocks,
            rows // PAIR,
            size // LANES,
        )
        full = exchange(grad, worker, sizes)
        return precondition(
            full, worker, row_extent, col_extent, fact_left, fact_right, root_left, root_right
        )

    return jax.shard_map(
        local,
        mesh=mesh,
        in_specs=placed,
        out_specs=(P("group", "dp", None), P("group", "dp", None), P("group", None, None)),
        check_vma=False,
    )
```

```python
import functools

import jax
import jax.numpy as jnp
from jax import lax
from jax.experimental import pallas as pl
from jax.experimental.pallas import tpu as pltpu
from jax.sharding import PartitionSpec as P

MESH = pl.DeviceIdType.MESH
LANES = 128
PAIR = 2
ROW_GROUPS = 3
RING = 4
SQUARE = 8
VMEM_BYTES = 60 * 1024 * 1024


def split_rank(rank):
    tile = lax.div(rank * 11, 32)
    return tile, rank - ROW_GROUPS * tile


def exchange_kernel(
    sizes,
    worker_hbm,
    grad_ref,
    full_ref,
    worker_ref,
    recv_ref,
    slot_ref,
    chosen_ref,
    worker_sem,
    ready_sem,
    rs_send,
    rs_recv,
    z_send,
    z_recv,
    ag_send,
    ag_recv,
):
    ranks, groups, blocks, pairs, tiles = sizes
    pieces = tiles * ROW_GROUPS
    slots = full_ref.shape[1]
    my_rank = lax.axis_index("dp")
    my_group = lax.axis_index("group")
    pltpu.make_async_copy(worker_hbm, worker_ref, worker_sem).start()
    barrier = pltpu.get_barrier_semaphore()

    def greet_rank(step, carry):
        pl.semaphore_signal(
            barrier,
            inc=1,
            device_id=(lax.rem(my_rank + step, ranks), my_group),
            device_id_type=MESH,
        )
        return carry

    row_first = SQUARE * lax.div(my_group, SQUARE)
    place = lax.rem(my_group, SQUARE)

    def in_row(step):
        return row_first + lax.rem(place + step, SQUARE)

    def in_column(step):
        return lax.rem(my_group + SQUARE * step, groups)

    def signal(semaphore, member):
        pl.semaphore_signal(
            semaphore, inc=1, device_id=(my_rank, member), device_id_type=MESH
        )

    def greet_row(step, carry):
        signal(barrier, in_row(step))
        return carry

    rows = groups // SQUARE
    lax.fori_loop(1, ranks, greet_rank, 0)
    lax.fori_loop(1, SQUARE, greet_row, 0)
    signal(barrier, in_column(1))
    signal(barrier, in_column(rows - 1))
    pl.semaphore_wait(barrier, ranks + SQUARE)

    def piece_rows(rank, half):
        tile, row_group = split_rank(rank)
        first = PAIR * (2 * row_group + half)
        lanes = pl.multiple_of(tile * LANES, LANES)
        return grad_ref.at[pl.ds(first, PAIR), :, pl.ds(lanes, LANES)]

    def when_held(rank, half, act):
        held = rank < pieces
        if half:
            held = held & (split_rank(rank)[1] < ROW_GROUPS - 1)

        @pl.when(held)
        def _():
            act()

    def scatter_each(half, act):
        def step_to(step, carry):
            target = lax.rem(my_rank + step, ranks)

            def go():
                act(
                    pltpu.make_async_remote_copy(
                        src_ref=piece_rows(target, half),
                        dst_ref=recv_ref.at[half, my_rank],
                        send_sem=rs_send.at[half, target],
                        recv_sem=rs_recv.at[half, my_rank],
                        device_id=(target, my_group),
                        device_id_type=MESH,
                    )
                )

            when_held(target, half, go)
            return carry

        lax.fori_loop(1, ranks, step_to, 0)

    halves = range(2)
    def scatter_start(half):
        scatter_each(half, lambda copy: copy.start())
        own = pltpu.make_async_copy(
            piece_rows(my_rank, half), recv_ref.at[half, my_rank], rs_recv.at[half, my_rank]
        )
        when_held(my_rank, half, own.start)

    scatter_start(0)

    depth = PAIR * blocks
    place_rows = PAIR * slots * groups

    def lay_out_places():
        lane = lax.broadcasted_iota(jnp.int32, (8, depth), 1)
        block_of = lax.rem(lane, blocks)

        def lay_out(block, held_by):
            return jnp.where(block_of == block, worker_ref[block], held_by)

        held_by = lax.fori_loop(0, blocks, lay_out, jnp.zeros_like(lane), unroll=8)

        def count_earlier(block, order):
            same = (held_by == worker_ref[block]) & (block_of > block)
            return order + same.astype(jnp.int32)

        order = lax.fori_loop(0, blocks, count_earlier, jnp.zeros_like(lane), unroll=8)
        place = PAIR * (slots * held_by + order) + lane // blocks
        row = lax.broadcasted_iota(jnp.int32, (place_rows, depth), 0)
        chosen_ref[...] = jnp.where(row == place[0:1], 1.0, 0.0).astype(jnp.bfloat16)

    rounds = rows // 2

    def tell(index):
        signal(ready_sem.at[index], in_column(1))
        signal(ready_sem.at[index], in_column(rows - 1))

    def hear(index):
        pl.semaphore_wait(ready_sem.at[index], 2)

    tell(0)
    pltpu.make_async_copy(worker_hbm, worker_ref, worker_sem).wait()
    when_held(my_rank, 0, lay_out_places)
    for index in range(1, rounds):
        hear(index - 1)
        tell(index)
    scatter_each(0, lambda copy: copy.wait_send())
    scatter_start(1)

    def spread_copy(half, target):
        return pltpu.make_async_remote_copy(
            src_ref=slot_ref.at[half, target],
            dst_ref=landing(half),
            send_sem=z_send.at[half],
            recv_sem=z_recv.at[half],
            device_id=(my_rank, target),
            device_id_type=MESH,
        )

    def landing(half):
        tile, row_group = split_rank(my_rank)
        return full_ref.at[tile, :, my_group, 2 * row_group + half]

    def spread(half):
        total = jnp.zeros((PAIR, blocks, LANES), jnp.float32)
        for step in range(ranks):
            source = lax.rem(my_rank + (ranks - step), ranks)
            arrived = recv_ref.at[half, source]
            pltpu.make_async_copy(arrived, arrived, rs_recv.at[half, source]).wait()
            total = total + recv_ref[half, source].astype(jnp.float32)
        total = total.reshape(depth, LANES).astype(jnp.bfloat16)
        placed = jnp.dot(chosen_ref[...], total, preferred_element_type=jnp.float32)
        slot_ref.at[half].reshape(place_rows, LANES)[...] = placed.astype(jnp.bfloat16)

        def spread_start(hop, carry):
            reach = groups // 2 - (hop + 1) // 2
            target = lax.rem(
                my_group + jnp.where(lax.rem(hop, 2) == 0, reach, groups - reach), groups
            )
            spread_copy(half, target).start()
            return carry

        lax.fori_loop(0, groups - 1, spread_start, 0)
        pltpu.make_async_copy(
            slot_ref.at[half, my_group], landing(half), z_recv.at[half]
        ).start()

    def spread_wait(half):
        tile, row_group = split_rank(my_rank)
        mine = full_ref.at[tile, :, :, 2 * row_group + half]
        pltpu.make_async_copy(mine, mine, z_recv.at[half]).wait()

    def spread_finish(half):
        sent = slot_ref.at[half, pl.ds(0, groups - 1)]
        pltpu.make_async_copy(sent, sent, z_send.at[half]).wait()

    hear(rounds - 1)
    for half in halves:
        when_held(my_rank, half, functools.partial(spread, half))

    side = RING
    my_x, my_y = my_rank // side, lax.rem(my_rank, side)
    chunks = [(slot, half) for half in halves for slot in range(slots)]

    def rank_at(slot, first, second):
        first, second = lax.rem(first, side), lax.rem(second, side)
        return side * first + second if slot == 0 else side * second + first

    def relay_copy(slot, half, source, target, index):
        tile, row_group = split_rank(source)
        piece = full_ref.at[tile, slot, :, 2 * row_group + half]
        return pltpu.make_async_remote_copy(
            src_ref=piece,
            dst_ref=piece,
            send_sem=ag_send.at[slot, half, index],
            recv_sem=ag_recv.at[slot, half, source],
            device_id=(target, my_group),
            device_id_type=MESH,
        )

    def relays(slot, half):
        first, second = (my_x, my_y) if slot == 0 else (my_y, my_x)
        at = functools.partial(rank_at, slot)
        ahead = (slot + half) % 2 == 0
        onward = (side - 1, 1) if ahead else (1, side - 1)
        lines = (0, 1, side - 1, side // 2)
        moves = {"own": [], "first": [], "second": [], "third": [], "last": []}
        me = at(first, second)
        moves["own"] = [
            (me, at(first + 1, second)),
            (me, at(first + side - 1, second)),
            (me, at(first, second + 1)),
            (me, at(first, second + side - 1)),
        ]
        for line in (1, side - 1):
            source = at(first + line, second)
            targets = [at(first, second + 1), at(first, second + side - 1)]
            if line == onward[0]:
                targets = [at(first + onward[1], second)] + targets
            moves["first"].append((source, targets))
        source = at(first + side // 2, second)
        moves["second"].append((source, [at(first, second + 1), at(first, second + side - 1)]))
        stages = ("first", "second", "second", "third")
        for line, stage in zip(lines, stages):
            for turn in (1, side - 1):
                source = at(first + line, second + turn)
                targets = [at(first, second + onward[1])] if turn == onward[0] else []
                moves[stage].append((source, targets))
            moves["last"].append((at(first + line, second + side // 2), []))
        return moves

    plans = {chunk: relays(*chunk) for chunk in chunks}
    started = {chunk: [] for chunk in chunks}

    def relay_start(slot, half, source, targets):
        sends = []
        for target in targets:
            index = len(started[slot, half])
            started[slot, half].append((source, target))
            sends.append(relay_copy(slot, half, source, target, index))
        when_held(source, half, lambda: [copy.start() for copy in sends])

    def relay_own(half):
        for slot in range(slots):
            moves = plans[slot, half]["own"]
            relay_start(slot, half, moves[0][0], [target for _, target in moves])

    def relay_on(stage, half):
        for slot in range(slots):
            for source, targets in plans[slot, half][stage]:
                arrival = relay_copy(slot, half, source, my_rank, 0)
                when_held(source, half, arrival.wait_recv)
                if targets:
                    relay_start(slot, half, source, targets)

    when_held(my_rank, 0, functools.partial(spread_wait, 0))
    relay_own(0)
    relay_on("first", 0)
    when_held(my_rank, 1, functools.partial(spread_wait, 1))
    relay_own(1)
    for stage, half in (
        ("second", 0),
        ("first", 1),
        ("third", 0),
        ("second", 1),
        ("third", 1),
        ("last", 0),
        ("last", 1),
    ):
        relay_on(stage, half)

    scatter_each(1, lambda copy: copy.wait_send())
    for half in halves:
        when_held(my_rank, half, functools.partial(spread_finish, half))
    for slot, half in chunks:
        for index, (source, target) in enumerate(started[slot, half]):
            sent = relay_copy(slot, half, source, target, index)
            when_held(source, half, sent.wait_send)


def exchange(grad, worker, sizes):
    ranks, groups, blocks, pairs, tiles = sizes
    slots = 2
    return pl.pallas_call(
        functools.partial(exchange_kernel, sizes),
        out_shape=jax.ShapeDtypeStruct(
            (tiles, slots, groups, pairs, PAIR, LANES), jnp.bfloat16
        ),
        in_specs=[
            pl.BlockSpec(memory_space=pl.ANY),
            pl.BlockSpec(memory_space=pl.ANY),
        ],
        out_specs=pl.BlockSpec(memory_space=pltpu.VMEM),
        scratch_shapes=[
            pltpu.SMEM((blocks,), jnp.int32),
            pltpu.VMEM((2, ranks, PAIR, blocks, LANES), jnp.bfloat16),
            pltpu.VMEM((2, groups, slots, PAIR, LANES), jnp.bfloat16),
            pltpu.VMEM((PAIR * slots * groups, PAIR * blocks), jnp.bfloat16),
            pltpu.SemaphoreType.DMA,
            pltpu.SemaphoreType.REGULAR((groups // SQUARE // 2,)),
            pltpu.SemaphoreType.DMA((2, ranks)),
            pltpu.SemaphoreType.DMA((2, ranks)),
            pltpu.SemaphoreType.DMA((2,)),
            pltpu.SemaphoreType.DMA((2,)),
            pltpu.SemaphoreType.DMA((slots, 2, ranks)),
            pltpu.SemaphoreType.DMA((slots, 2, ranks)),
        ],
        compiler_params=pltpu.CompilerParams(
            collective_id=0, has_side_effects=True, vmem_limit_bytes=VMEM_BYTES
        ),
    )(worker, grad)


def update_kernel(
    worker_ref,
    row_extent_ref,
    col_extent_ref,
    full_ref,
    fact_left_ref,
    fact_right_ref,
    root_left_ref,
    root_right_ref,
    new_left_ref,
    new_right_ref,
    update_ref,
    grad_ref,
):
    slot = pl.program_id(0)
    my_rank = lax.axis_index("dp")
    my_group = lax.axis_index("group")
    blocks = worker_ref.shape[0]
    tiles, _, groups, pairs, _, _ = full_ref.shape
    size = root_left_ref.shape[1]
    own = fact_left_ref.shape[1]

    def find(block, carry):
        seen, rows, cols = carry
        mine = worker_ref[block] == my_group
        hit = mine & (seen == slot)
        rows = jnp.where(hit, row_extent_ref[block], rows)
        cols = jnp.where(hit, col_extent_ref[block], cols)
        return seen + mine.astype(jnp.int32), rows, cols

    zero = jnp.int32(0)
    _, row_limit, col_limit = lax.fori_loop(0, blocks, find, (zero, zero, zero), unroll=True)

    row = lax.broadcasted_iota(jnp.int32, (size, LANES), 0)
    lane = lax.broadcasted_iota(jnp.int32, (size, LANES), 1)
    for tile in range(tiles):
        part = full_ref.at[tile, 0].reshape(size, LANES)[...]
        inside = (row < row_limit) & (tile * LANES + lane < col_limit)
        grad_ref[:, tile * LANES : (tile + 1) * LANES] = jnp.where(
            inside, part.astype(jnp.float32), 0.0
        ).astype(jnp.bfloat16)
    grad = grad_ref[...]

    mixed = jnp.dot(grad, root_right_ref[0], preferred_element_type=jnp.float32)
    product = jnp.dot(
        root_left_ref[0], mixed.astype(jnp.bfloat16), preferred_element_type=jnp.float32
    )
    out_row = lax.broadcasted_iota(jnp.int32, (size, size), 0)
    out_col = lax.broadcasted_iota(jnp.int32, (size, size), 1)
    inside = (out_row < row_limit) & (out_col < col_limit)
    update_ref[0] = jnp.where(inside, product, 0.0).astype(jnp.bfloat16)

    start = my_rank * own
    pick = lax.broadcasted_iota(jnp.int32, (size, LANES), 0) == start + lane
    pick = jnp.where(pick & (lane < own), 1.0, 0.0).astype(jnp.bfloat16)
    own_cols = jnp.dot(grad, pick, preferred_element_type=jnp.float32).astype(jnp.bfloat16)
    own_rows = lax.dot_general(
        pick, grad, (((0,), (0,)), ((), ())), preferred_element_type=jnp.float32
    ).astype(jnp.bfloat16)
    left = lax.dot_general(
        own_rows, grad, (((1,), (1,)), ((), ())), preferred_element_type=jnp.float32
    )
    right = lax.dot_general(
        own_cols, grad, (((0,), (0,)), ((), ())), preferred_element_type=jnp.float32
    )
    new_left_ref[0] = fact_left_ref[0] + left[:own]
    new_right_ref[0] = fact_right_ref[0] + right[:own]


def precondition(full, worker, row_extent, col_extent, fact_left, fact_right, root_left, root_right):
    slots, own, size = fact_left.shape
    tiles, _, groups, pairs, _, _ = full.shape
    smem = pl.BlockSpec(memory_space=pltpu.SMEM)
    fact = pl.BlockSpec((1, own, size), lambda slot: (slot, 0, 0))
    root = pl.BlockSpec((1, size, size), lambda slot: (slot, 0, 0))
    return pl.pallas_call(
        update_kernel,
        grid=(slots,),
        out_shape=(
            jax.ShapeDtypeStruct(fact_left.shape, jnp.float32),
            jax.ShapeDtypeStruct(fact_right.shape, jnp.float32),
            jax.ShapeDtypeStruct(root_left.shape, jnp.bfloat16),
        ),
        in_specs=[
            smem,
            smem,
            smem,
            pl.BlockSpec(
                (tiles, 1, groups, pairs, PAIR, LANES), lambda slot: (0, slot, 0, 0, 0, 0)
            ),
            fact,
            fact,
            root,
            root,
        ],
        out_specs=(fact, fact, root),
        scratch_shapes=[pltpu.VMEM((size, size), jnp.bfloat16)],
        compiler_params=pltpu.CompilerParams(vmem_limit_bytes=VMEM_BYTES),
    )(worker, row_extent, col_extent, full, fact_left, fact_right, root_left, root_right)


def solution(mesh):
    placed = (
        P("dp", None, "group", None),
        P(),
        P(),
        P(),
        P("group", "dp", None),
        P("group", "dp", None),
        P("group", None, None),
        P("group", None, None),
    )

    def local(grad_parts, row_extent, col_extent, worker, fact_left, fact_right, root_left, root_right):
        grad = jnp.transpose(grad_parts[0], (1, 0, 2))
        rows, blocks, size = grad.shape
        sizes = (
            mesh.shape["dp"],
            mesh.shape["group"],
            blocks,
            rows // PAIR,
            size // LANES,
        )
        full = exchange(grad, worker, sizes)
        return precondition(
            full, worker, row_extent, col_extent, fact_left, fact_right, root_left, root_right
        )

    return jax.shard_map(
        local,
        mesh=mesh,
        in_specs=placed,
        out_specs=(P("group", "dp", None), P("group", "dp", None), P("group", None, None)),
        check_vma=False,
    )
```
